32 devices in a mesh: vocab: 8 (over z, x), fsdp: 4 (over y, core).
Axes of the slice: x: 2, y: 2, z: 4, core: 2. Of those that a mesh axis runs over, the one named last changes fastest.
Arguments:
- hidden: bfloat16 [16384, 2048], P(('vocab', 'fsdp')), may hold values from -100 to 100
- head_weight: bfloat16 [262144, 2048], P(('vocab', 'fsdp')), may hold values from -2.5 to 2.5
- language_blocks: int32 [256, 6], replicated, may hold values from 0 to 7, as said below
- language_owner: int32 [256], replicated, may hold values from 0 to 255, each once
- token_language: int32 [16384, 1], P(('vocab', 'fsdp')), may hold values from 0 to 255; in each aligned block of 512 rows (0 to 511, 512 to 1023, ...) at most 4 rows name the same one
- labels: int32 [16384], P(('vocab', 'fsdp')), may hold values from 0 to 767
- loss_weight: bfloat16 [16384], P(('vocab', 'fsdp')), may hold values from 1 to 16
Outputs:
- hidden_grad: bfloat16 [16384, 2048], P(('vocab', 'fsdp'))
- token_loss: bfloat16 [16384], P(('vocab', 'fsdp'))
- head_grad: bfloat16 [262144, 2048], P(('vocab', 'fsdp'))
The draws below stay inside these ranges and needn't reach their ends.
Inputs may be any that keep to these rules, and one draw needn't show every extreme that they name: `language_blocks`: each row names 6 different blocks. `language_owner`: each language slot is named by exactly one language. `token_language`: in each aligned group of 512 tokens no language is named more than 4 times, a bound that some block reaches in some or all groups.
All inputs are finite; a program needn't handle non-finite values.
Results may differ from the reference program's by a relative error of at most 0.0049.
Values may be sent and summed in bfloat16 or wider, within the bound.
A program may use at most 192 MiB of HBM per device.

```python
import math
import jax
import jax.numpy as jnp
import numpy as np
from jax import lax

D = 2048
BLOCK = 128
LANGS = 256
SB = 8
LB = 6
TOK_DEV = 512
CAP = 4
TOKENS = 16384
VOCAB = 262144
N_VOCAB = 8
N_FSDP = 4


def draw_hidden(key, part):
    noise_key = jax.random.fold_in(key, 11)
    values = jax.random.truncated_normal(noise_key, -5.0, 5.0, (TOKENS, D), jnp.float32)
    return values.astype(jnp.bfloat16)


def draw_head_weight(key, part):
    noise_key = jax.random.fold_in(key, 21)
    values = jax.random.truncated_normal(noise_key, -5.0, 5.0, (VOCAB, D), jnp.float32) * (3.0 / math.sqrt(D))
    return values.astype(jnp.bfloat16)


def draw_language_blocks(key, part):
    row_keys = jax.random.split(jax.random.fold_in(key, 31), LANGS)
    chosen = jax.vmap(lambda subkey: jax.random.permutation(subkey, SB)[:LB])(row_keys)
    return chosen.astype(jnp.int32)


def with_ends(entries, own_key, least, largest):
    place = [jax.random.randint(jax.random.fold_in(own_key, axis), (), 0, length) for axis, length in enumerate(entries.shape)]
    widest = entries.shape.index(max(entries.shape))
    neighbour = place[:widest] + [(place[widest] + 1) % entries.shape[widest]] + place[widest + 1:]
    return entries.at[tuple(place)].set(least).at[tuple(neighbour)].set(largest)


def steps_of(rng, dims, shards, low, top_value):
    gain, own = 1.0, jax.random.fold_in(rng, 6)
    for dim, shards_of in shards:
        steps = jnp.exp(jax.random.uniform(jax.random.fold_in(own, dim), (shards_of,), jnp.float32, low / len(shards), top_value / len(shards)))
        gain = gain * jnp.repeat(steps, dims[dim] // shards_of).reshape([-1 if axis == dim else 1 for axis in range(len(dims))])
    return gain


def shared_out(rng, own, number, rows, count, top, most, lean):
    order = jax.random.permutation(rng, count)
    packed, common = shares(count, rows * top, most, lean, True), shares(count, rows * top, most, lean, False)
    places = jnp.arange(count)

    def named(sizes, turn):
        used = int((sizes > 0).sum())
        fixed = max(1, used // 4)
        passed = fixed + (places - fixed + turn * (used - fixed)) % max(1, count - fixed)
        return jnp.zeros((count,), jnp.int32).at[order[jnp.where(places < fixed, places, passed)]].set(jnp.asarray(sizes, jnp.int32))

    sizes = jnp.where(number % 4 == 0, named(packed, number // 4), named(common, number - number // 4 - 1))
    mixed = jax.random.permutation(jax.random.fold_in(own, 3), count)
    source_of, sink = mixed[0:count // 2 * 2:2], mixed[1:count // 2 * 2:2]
    room = jnp.minimum(sizes[source_of] - 1, most - sizes[sink]) // 2
    room = jnp.where((source_of == order[0]) | (sink == order[0]) | (sizes[sink] == 0), 0, jnp.maximum(room, 0))
    passed = jax.random.randint(jax.random.fold_in(own, 4), (count // 2,), 0, 1 << 20) % (room + 1)
    sizes = sizes.at[source_of].add(-passed).at[sink].add(passed)
    members = jnp.searchsorted(jnp.cumsum(sizes), jnp.arange(rows * top), side="right").astype(jnp.int32)
    grid = members.reshape(top, rows).T
    grid = grid[jax.random.permutation(jax.random.fold_in(own, 1), rows)]
    turn = jax.random.randint(jax.random.fold_in(own, 2), (rows, 1), 0, top)
    return jnp.take_along_axis(grid, (jnp.arange(top)[None, :] + turn) % top, axis=1)


def shares(amount, total, limit, skew, full):
    weights = [(1 << 20) // math.isqrt(grade ** skew) + 1 for grade in range(1, amount + 1)]
    largest = limit if full else min(limit, max(-(-total // amount), total * weights[0] // sum(weights)))
    least = 1 if total - largest >= amount - 1 else 0
    given, spare = [largest] + [least] * (amount - 1), total - largest - least * (amount - 1)
    while spare > 0:
        movable = [i for i in range(1, amount) if given[i] < largest] or [i for i in range(1, amount) if given[i] < limit]
        pool, remaining = sum([weights[i] for i in movable]), spare
        for i in movable:
            more = min(limit - given[i], max(1, remaining * weights[i] // pool), spare)
            given[i] = given[i] + more
            spare = spare - more
    return np.array(given)


def setup_inputs(seed: int = 0) -> dict:
    seeds = jax.random.split(jax.random.key(seed), 8)
    hidden = draw_hidden(jax.random.fold_in(seeds[7], 71), 0)
    head_weight = draw_head_weight(jax.random.fold_in(seeds[7], 71), 0)
    language_blocks = draw_language_blocks(jax.random.fold_in(seeds[7], 71), 0)
    language_owner = jax.random.permutation(seeds[3], LANGS).astype(jnp.int32)
    token_language_keys = jax.random.split(jax.random.fold_in(seeds[4], 1), TOKENS // TOK_DEV)
    token_language_turns = jax.random.permutation(jax.random.fold_in(seeds[4], 3), TOKENS // TOK_DEV)
    token_language = jax.vmap(lambda own, number: shared_out(jax.random.fold_in(seeds[4], 2), own, number, TOK_DEV, LANGS, 1, CAP, 2))(token_language_keys, token_language_turns).reshape((TOKENS, 1))
    labels = with_ends(jax.random.randint(seeds[5], (TOKENS,), 0, LB * BLOCK), jax.random.fold_in(seeds[5], 1), 0, (LB * BLOCK) - 1).astype(jnp.int32)
    loss_weight = jnp.clip(jnp.exp(math.log(16.0) - 2.7725887 * jax.random.uniform(seeds[6], (TOKENS,), jnp.float32) ** steps_of(seeds[6], (TOKENS,), ((0, 32),), -0.2, 0.2)), 1.0, 16.0).astype(jnp.bfloat16)
    return dict(hidden=hidden, head_weight=head_weight, language_blocks=language_blocks, language_owner=language_owner, token_language=token_language, labels=labels, loss_weight=loss_weight)


SMOOTH = 0.1


def smoothed_loss(logits, targets, weights):
    columns = logits.shape[1]
    row_max = jnp.max(logits, axis=1, keepdims=True)
    shifted = logits - row_max
    log_probs = shifted - jnp.log(jnp.sum(jnp.exp(shifted), axis=1, keepdims=True))
    onehot = (lax.broadcasted_iota(jnp.int32, logits.shape, 1) == targets[:, None]).astype(jnp.float32)
    losses = -(1.0 - SMOOTH) * jnp.sum(onehot * log_probs, axis=1) - (SMOOTH / columns) * jnp.sum(log_probs, axis=1)
    grads = weights.astype(jnp.float32)[:, None] * (jnp.exp(log_probs) - (1.0 - SMOOTH) * onehot - SMOOTH / columns)
    return losses.astype(jnp.bfloat16), grads.astype(jnp.bfloat16)


def slot_work(token_rows, weights, targets, slot_weights, blocks):
    candidates = jnp.take(slot_weights, blocks, axis=0).reshape(LB * BLOCK, D)
    logits = lax.dot_general(token_rows, candidates, (((1,), (1,)), ((), ())), preferred_element_type=jnp.float32)
    losses, grads = smoothed_loss(logits, targets, weights)
    row_grads = jnp.dot(grads, candidates, preferred_element_type=jnp.float32).astype(jnp.bfloat16)
    cand_grads = lax.dot_general(grads, token_rows, (((0,), (0,)), ((), ())), preferred_element_type=jnp.float32)
    slab_grads = jnp.zeros((SB, BLOCK, D), jnp.float32).at[blocks].add(cand_grads.reshape(LB, BLOCK, D))
    return row_grads, losses, slab_grads.astype(jnp.bfloat16)


def reference(hidden, head_weight, language_blocks, language_owner, token_language, labels, loss_weight):
    devices = N_VOCAB * N_FSDP
    language = token_language[:, 0]
    slot_ids = jnp.take(language_owner, language, axis=0)
    grouped = language.reshape(devices, TOK_DEV)
    positions = jnp.arange(TOK_DEV, dtype=jnp.int32)
    earlier = (grouped[:, :, None] == grouped[:, None, :]) & (positions[None, None, :] < positions[None, :, None])
    rank_in_group = jnp.sum(earlier.astype(jnp.int32), axis=2).reshape(TOKENS)
    source = jnp.arange(TOKENS, dtype=jnp.int32) // TOK_DEV
    position = source * CAP + rank_in_group
    places = devices * CAP
    language_of = jnp.zeros((LANGS,), jnp.int32).at[language_owner].set(jnp.arange(LANGS, dtype=jnp.int32))
    slab_weights = head_weight.reshape(LANGS, SB, BLOCK, D)
    token_ids = jnp.arange(TOKENS, dtype=jnp.int32)

    def slot_step(running, slot_items):
        hidden_grad, token_loss = running
        slot_index, slot_weights = slot_items
        target_place = jnp.where(slot_ids == slot_index, position, places)
        row_index = jnp.full((places,), TOKENS, jnp.int32).at[target_place].set(token_ids, mode="drop")
        token_rows = jnp.take(hidden, row_index, axis=0, mode="fill", fill_value=0)
        weights = jnp.take(loss_weight, row_index, axis=0, mode="fill", fill_value=0)
        targets = jnp.take(labels, row_index, axis=0, mode="fill", fill_value=0)
        blocks = jnp.take(language_blocks, language_of[slot_index], axis=0)
        row_grads, losses, slab_grads = slot_work(token_rows, weights, targets, slot_weights, blocks)
        hidden_grad = hidden_grad.at[row_index].set(row_grads, mode="drop")
        token_loss = token_loss.at[row_index].set(losses, mode="drop")
        return (hidden_grad, token_loss), slab_grads

    start_state = (jnp.zeros((TOKENS, D), jnp.bfloat16), jnp.zeros((TOKENS,), jnp.bfloat16))
    (hidden_grad, token_loss), head_grads = lax.scan(slot_step, start_state, (jnp.arange(LANGS, dtype=jnp.int32), slab_weights))
    return hidden_grad, token_loss, head_grads.reshape(VOCAB, D)
```

```python
import functools

import jax
import jax.numpy as jnp
from jax import lax
from jax.experimental import pallas as pl
from jax.experimental.pallas import tpu as pltpu
from jax.sharding import PartitionSpec as P

BLOCK = 128
SB = 8
LB = 6
CAP = 4
SMOOTH = 0.1
AXES = ("vocab", "fsdp")
EXTRA = 128
VMEM = 56 * 1024 * 1024


def one_hot(condition):
    return condition.astype(jnp.float32).astype(jnp.bfloat16)


def placing(place_row, chunk, chunks, per, rows):
    index = lax.broadcasted_iota(jnp.int32, (rows, 1), 0)
    place = (index // per) * (per * chunks) + chunk * per + index % per
    return one_hot(place == place_row)


def dispatch_kernel(chunks, per, lang_col, lang_row, owner_col, hidden, meta, place_out, *outs):
    tokens = hidden.shape[0]
    languages = owner_col.shape[0]
    language_ids = lax.broadcasted_iota(jnp.int32, (languages, tokens), 0)
    slot = jnp.sum(
        jnp.where(language_ids == lang_row[...], owner_col[...], 0), axis=0, keepdims=True
    )
    before = lax.broadcasted_iota(jnp.int32, (tokens, tokens), 0) < lax.broadcasted_iota(
        jnp.int32, (tokens, tokens), 1
    )
    same = lang_col[...] == lang_row[...]
    rank = jnp.sum(jnp.where(same & before, 1, 0), axis=0, keepdims=True)
    place = slot * CAP + rank
    place_out[...] = place
    features = hidden.shape[1]
    for chunk, out in enumerate(outs):
        picks = placing(place, chunk, chunks, per, out.shape[0])
        out[:, :features] = jnp.dot(
            picks, hidden[...], preferred_element_type=jnp.float32
        ).astype(jnp.bfloat16)
        out[:, features:] = jnp.dot(
            picks, meta[...], preferred_element_type=jnp.float32
        ).astype(jnp.bfloat16)


def slots_kernel(slots, first, blocks, incoming, slab, back, rows_out, grads_out, held):
    step = pl.program_id(0)
    total = incoming.shape[0]
    rows = total // slots
    features = slab.shape[1]
    columns = slab.shape[0]
    per = CAP * slots
    if slots > 1:
        wanted = lax.broadcasted_iota(jnp.int32, (rows, 1), 0)
        wanted = (wanted // CAP) * per + step * CAP + wanted % CAP
        picks = one_hot(wanted == lax.broadcasted_iota(jnp.int32, (rows, total), 1))
        rows_out[...] = jnp.dot(
            picks, incoming[:, :features], preferred_element_type=jnp.float32
        ).astype(jnp.bfloat16)
        extra = jnp.dot(picks, incoming[:, features:], preferred_element_type=jnp.float32)
    else:
        rows_out[...] = incoming[:, :features]
        extra = incoming[:, features:].astype(jnp.float32)
    weights = extra[:, 0:1]
    targets = (extra[:, 1:2] * BLOCK + extra[:, 2:3]).astype(jnp.int32)
    column = lax.broadcasted_iota(jnp.int32, (1, columns), 1)
    listed = jnp.full((1, columns), -1, jnp.int32)
    for j in range(LB):
        named = blocks[(first + step) * LB + j]
        listed = jnp.where(column // BLOCK == named, j * BLOCK + column % BLOCK, listed)
    used = listed >= 0
    logits = lax.dot_general(
        rows_out[...], slab[...], (((1,), (1,)), ((), ())), preferred_element_type=jnp.float32
    )
    count = LB * BLOCK
    row_max = jnp.max(jnp.where(used, logits, -jnp.inf), axis=1, keepdims=True)
    shifted = jnp.where(used, logits - row_max, 0.0)
    powers = jnp.where(used, jnp.exp(shifted), 0.0)
    sums = jnp.sum(powers, axis=1, keepdims=True)
    log_sums = jnp.log(sums)
    is_target = listed == targets
    at_target = jnp.sum(jnp.where(is_target, shifted, 0.0), axis=1, keepdims=True) - log_sums
    all_of_them = jnp.sum(shifted, axis=1, keepdims=True) - count * log_sums
    losses = -(1.0 - SMOOTH) * at_target - SMOOTH / count * all_of_them
    grads = weights * (
        powers * (1.0 / sums) - jnp.where(is_target, 1.0 - SMOOTH, 0.0) - SMOOTH / count
    )
    grads = jnp.where(used, grads, 0.0).astype(jnp.bfloat16)
    grads_out[...] = grads
    row_grads = jnp.dot(grads, slab[...], preferred_element_type=jnp.float32).astype(jnp.bfloat16)
    lane = lax.broadcasted_iota(jnp.int32, (rows, EXTRA), 1)
    tail = jnp.where(lane == 0, losses, 0.0).astype(jnp.bfloat16)
    if slots > 1:
        here = pl.ds(pl.multiple_of(step * rows, rows), rows)
        held[here, :features] = row_grads
        held[here, features:] = tail

        @pl.when(step == slots - 1)
        def _():
            index = lax.broadcasted_iota(jnp.int32, (total, 1), 0)
            source = ((index % per) // CAP) * rows + (index // per) * CAP + index % CAP
            spread = one_hot(source == lax.broadcasted_iota(jnp.int32, (total, total), 1))
            back[...] = jnp.dot(spread, held[...], preferred_element_type=jnp.float32).astype(
                jnp.bfloat16
            )
    else:
        back[:, :features] = row_grads
        back[:, features:] = tail


def head_kernel(chunks, slots, *refs):
    out = refs[-1]
    step = pl.program_id(0)
    for chunk in range(chunks):
        rows, grads = refs[2 * chunk], refs[2 * chunk + 1]

        @pl.when(step // slots == chunk)
        def _():
            out[...] = lax.dot_general(
                grads[...], rows[...], (((0,), (0,)), ((), ())),
                preferred_element_type=jnp.float32,
            ).astype(jnp.bfloat16)


def combine_kernel(chunks, per, place, *refs):
    returned, (hidden_out, loss_out) = refs[:chunks], refs[chunks:]
    features = hidden_out.shape[1]
    total, losses = None, None
    for chunk, part in enumerate(returned):
        picks = placing(place[...], chunk, chunks, per, part.shape[0])
        rows = lax.dot_general(
            picks, part[:, :features], (((0,), (0,)), ((), ())),
            preferred_element_type=jnp.float32,
        )
        loss = lax.dot_general(
            part[:, features:], picks, (((0,), (0,)), ((), ())),
            preferred_element_type=jnp.float32,
        )
        total = rows if total is None else total + rows
        losses = loss if losses is None else losses + loss
    hidden_out[...] = total.astype(jnp.bfloat16)
    loss_out[...] = losses[0:1, :].astype(jnp.bfloat16)


def shards(
    hidden, head_weight, language_blocks, language_owner, token_language, labels, loss_weight
):
    devices = lax.axis_size("vocab") * lax.axis_size("fsdp")
    languages = language_owner.shape[0]
    tokens, features = hidden.shape
    owned = languages // devices
    chunks = 2 if owned % 2 == 0 else 1
    slots = owned // chunks
    per = slots * CAP
    chunk_rows = devices * per
    slot_rows = devices * CAP
    slab_rows = SB * BLOCK
    width = features + EXTRA
    params = pltpu.CompilerParams(vmem_limit_bytes=VMEM)

    lane = lax.broadcasted_iota(jnp.int32, (tokens, EXTRA), 1)
    label_col = labels[:, None]
    parts = jnp.where(lane == 1, label_col // BLOCK, label_col % BLOCK)
    meta = jnp.where(
        lane == 0, loss_weight[:, None].astype(jnp.float32), parts.astype(jnp.float32)
    )
    meta = jnp.where(lane < 3, meta, 0.0).astype(jnp.bfloat16)
    place, *outgoing = pl.pallas_call(
        functools.partial(dispatch_kernel, chunks, per),
        out_shape=[jax.ShapeDtypeStruct((1, tokens), jnp.int32)]
        + [jax.ShapeDtypeStruct((chunk_rows, width), jnp.bfloat16)] * chunks,
        compiler_params=params,
        cost_estimate=pl.CostEstimate(
            flops=2 * chunks * chunk_rows * tokens * width, bytes_accessed=8 << 20, transcendentals=0
        ),
    )(token_language, token_language.reshape(1, tokens), language_owner[:, None], hidden, meta)

    self_index = lax.axis_index(AXES)
    own_slots = self_index * owned + jnp.arange(owned, dtype=jnp.int32)
    owns = (own_slots[:, None] == language_owner[None, :]).astype(jnp.int32)
    blocks = jnp.sum(owns[:, :, None] * language_blocks[None], axis=1).reshape(-1)

    def exchange(values):
        shaped = values.reshape(devices, per, width)
        return lax.all_to_all(shaped, AXES, split_axis=0, concat_axis=0, tiled=True).reshape(
            chunk_rows, width
        )

    incoming = [exchange(values) for values in outgoing]
    kept, returned = [], []
    for chunk in range(chunks):
        first = chunk * slots
        back, rows, grads = pl.pallas_call(
            functools.partial(slots_kernel, slots, first),
            out_shape=[
                jax.ShapeDtypeStruct((chunk_rows, width), jnp.bfloat16),
                jax.ShapeDtypeStruct((slots * slot_rows, features), jnp.bfloat16),
                jax.ShapeDtypeStruct((slots * slot_rows, slab_rows), jnp.bfloat16),
            ],
            grid_spec=pltpu.PrefetchScalarGridSpec(
                num_scalar_prefetch=1,
                grid=(slots,),
                in_specs=[
                    pl.BlockSpec((chunk_rows, width), lambda s, b: (0, 0)),
                    pl.BlockSpec((slab_rows, features), lambda s, b, first=first: (first + s, 0)),
                ],
                out_specs=[
                    pl.BlockSpec((chunk_rows, width), lambda s, b: (0, 0)),
                    pl.BlockSpec((slot_rows, features), lambda s, b: (s, 0)),
                    pl.BlockSpec((slot_rows, slab_rows), lambda s, b: (s, 0)),
                ],
                scratch_shapes=[pltpu.VMEM((chunk_rows, width), jnp.bfloat16)],
            ),
            compiler_params=params,
            cost_estimate=pl.CostEstimate(
                flops=4 * slots * slot_rows * slab_rows * features,
                bytes_accessed=2 * slots * slab_rows * features + (12 << 20),
                transcendentals=0,
            ),
        )(blocks, incoming[chunk], head_weight)
        kept += [rows, grads]
        returned.append(exchange(back))

    kept_specs = []
    for chunk in range(chunks):

        def at(s, chunk=chunk):
            return (jnp.clip(s - chunk * slots, 0, slots - 1), 0)

        kept_specs += [
            pl.BlockSpec((slot_rows, features), at),
            pl.BlockSpec((slot_rows, slab_rows), at),
        ]
    head_grad = pl.pallas_call(
        functools.partial(head_kernel, chunks, slots),
        out_shape=jax.ShapeDtypeStruct(head_weight.shape, jnp.bfloat16),
        grid=(owned,),
        in_specs=kept_specs,
        out_specs=pl.BlockSpec((slab_rows, features), lambda s: (s, 0)),
        compiler_params=params,
        cost_estimate=pl.CostEstimate(
            flops=2 * owned * slot_rows * slab_rows * features,
            bytes_accessed=2 * owned * slab_rows * features,
            transcendentals=0,
        ),
    )(*kept)
    hidden_grad, token_loss = pl.pallas_call(
        functools.partial(combine_kernel, chunks, per),
        out_shape=[
            jax.ShapeDtypeStruct((tokens, features), jnp.bfloat16),
            jax.ShapeDtypeStruct((1, tokens), jnp.bfloat16),
        ],
        compiler_params=params,
        cost_estimate=pl.CostEstimate(
            flops=2 * chunks * chunk_rows * tokens * width, bytes_accessed=8 << 20, transcendentals=0
        ),
    )(place, *returned)
    return hidden_grad, token_loss.reshape(tokens), head_grad


def solution(mesh):
    in_specs = (
        P(AXES, None),
        P(AXES, None),
        P(),
        P(),
        P(AXES, None),
        P(AXES),
        P(AXES),
    )
    out_specs = (P(AXES, None), P(AXES), P(AXES, None))
    return jax.shard_map(shards, mesh=mesh, in_specs=in_specs, out_specs=out_specs, check_vma=False)
```

```python
import functools

import jax
import jax.numpy as jnp
from jax import lax
from jax.experimental import pallas as pl
from jax.experimental.pallas import tpu as pltpu
from jax.sharding import PartitionSpec as P

BLOCK = 128
SB = 8
LB = 6
CAP = 4
SMOOTH = 0.1
AXES = ("vocab", "fsdp")
SIDE = 8
VMEM = 56 * 1024 * 1024
F32 = jnp.float32
BF16 = jnp.bfloat16


def one_hot(condition):
    return condition.astype(F32).astype(BF16)


def matmul(a, b, contract_a=1, contract_b=0):
    return lax.dot_general(
        a, b, (((contract_a,), (contract_b,)), ((), ())), preferred_element_type=F32
    )


def stack_rows(rows, width):
    line = lax.broadcasted_iota(jnp.int32, (SIDE, width), 0)
    total = jnp.zeros((SIDE, width), rows[0].dtype)
    for i, row in enumerate(rows):
        total = jnp.where(line == i, row, total)
    return total


def place_kernel(owned, lang_col, lang_row, owner_col, owner_row, label, weight, info, side):
    tokens = lang_row.shape[1]
    languages = owner_col.shape[0]
    slot_row = jnp.sum(
        jnp.where(
            lax.broadcasted_iota(jnp.int32, (languages, tokens), 0) == lang_row[...],
            owner_col[...],
            0,
        ),
        axis=0,
        keepdims=True,
    )
    slot_col = jnp.sum(
        jnp.where(
            lax.broadcasted_iota(jnp.int32, (tokens, languages), 1) == lang_col[...],
            owner_row[...],
            0,
        ),
        axis=1,
        keepdims=True,
    )
    before = lax.broadcasted_iota(jnp.int32, (tokens, tokens), 0) < lax.broadcasted_iota(
        jnp.int32, (tokens, tokens), 1
    )
    rank = jnp.sum(
        jnp.where((slot_col == slot_row) & before, 1, 0), axis=0, keepdims=True
    )
    dest = slot_row // owned
    position = jnp.sum(
        jnp.where((slot_col // owned == dest) & before, 1, 0), axis=0, keepdims=True
    )
    code = (slot_row - dest * owned) * CAP + rank + 1
    info[...] = stack_rows([dest, position], tokens)
    high = label[...] // BLOCK
    side[...] = stack_rows(
        [
            weight[...].astype(F32),
            high.astype(F32),
            (label[...] - high * BLOCK).astype(F32),
            code.astype(F32),
        ],
        tokens,
    ).astype(BF16)


def placing(info, capacity, rows):
    index = lax.broadcasted_iota(jnp.int32, (rows, 1), 0)
    return one_hot(index == info[0:1, :] * capacity + info[1:2, :])


def send_kernel(capacity, info, hidden, side, out_a, out_b, side_out):
    picks = placing(info, capacity, out_a.shape[0])
    split = out_a.shape[1]
    out_a[...] = matmul(picks, hidden[:, :split]).astype(BF16)
    out_b[...] = matmul(picks, hidden[:, split:]).astype(BF16)
    side_out[...] = matmul(side[...], picks, 1, 1)


def slot_picks(side, step, capacity, rows):
    buffer_rows = side.shape[1]
    index = lax.broadcasted_iota(jnp.int32, (rows, 1), 0)
    source = lax.broadcasted_iota(jnp.int32, (1, buffer_rows), 1) // capacity
    code = side[3:4, :].astype(jnp.int32) - 1
    where = jnp.where((code >= 0) & (code // CAP == step), source * CAP + code % CAP, -1)
    return one_hot(index == where)


def all_picks(side, owned, rows, capacity):
    buffer_rows = side.shape[1]
    index = lax.broadcasted_iota(jnp.int32, (owned * rows, 1), 0)
    source = lax.broadcasted_iota(jnp.int32, (1, buffer_rows), 1) // capacity
    code = side[3:4, :].astype(jnp.int32) - 1
    where = jnp.where(code >= 0, code // CAP * rows + source * CAP + code % CAP, -1)
    return one_hot(index == where)


def logits_kernel(capacity, side, incoming, slab, partial, rows_out):
    picks = slot_picks(side, pl.program_id(0), capacity, rows_out.shape[0])
    rows_out[...] = matmul(picks, incoming[...]).astype(BF16)
    partial[...] = matmul(rows_out[...], slab[...], 1, 1)


def loss_kernel(
    capacity, owned, blocks, side, incoming, slab, partial, rows_out, grads_out, back, loss_out, held
):
    step = pl.program_id(0)
    rows, columns = partial.shape
    picks = slot_picks(side, step, capacity, rows)
    rows_out[...] = matmul(picks, incoming[...]).astype(BF16)
    logits = partial[...] + matmul(rows_out[...], slab[...], 1, 1)
    extra = matmul(picks, side[...].astype(BF16), 1, 1)
    weights = extra[:, 0:1]
    targets = (extra[:, 1:2] * BLOCK + extra[:, 2:3]).astype(jnp.int32)
    column = lax.broadcasted_iota(jnp.int32, (1, columns), 1)
    listed = jnp.full((1, columns), -1, jnp.int32)
    for j in range(LB):
        named = blocks[step * LB + j]
        listed = jnp.where(column // BLOCK == named, j * BLOCK + column % BLOCK, listed)
    used = listed >= 0
    count = LB * BLOCK
    row_max = jnp.max(jnp.where(used, logits, -jnp.inf), axis=1, keepdims=True)
    shifted = jnp.where(used, logits - row_max, 0.0)
    powers = jnp.where(used, jnp.exp(shifted), 0.0)
    sums = jnp.sum(powers, axis=1, keepdims=True)
    log_sums = jnp.log(sums)
    is_target = listed == targets
    at_target = jnp.sum(jnp.where(is_target, shifted, 0.0), axis=1, keepdims=True) - log_sums
    all_of_them = jnp.sum(shifted, axis=1, keepdims=True) - count * log_sums
    losses = -(1.0 - SMOOTH) * at_target - SMOOTH / count * all_of_them
    grads = weights * (
        powers * (1.0 / sums) - jnp.where(is_target, 1.0 - SMOOTH, 0.0) - SMOOTH / count
    )
    grads = jnp.where(used, grads, 0.0).astype(BF16)
    grads_out[...] = grads
    here = pl.ds(pl.multiple_of(step * rows, rows), rows)
    held[here, :] = matmul(grads, slab[...]).astype(BF16)
    lane = lax.broadcasted_iota(jnp.int32, (rows, BLOCK), 1)
    tail = jnp.where(lane == 0, losses, 0.0).astype(BF16)
    line = matmul(tail, picks, 0, 0)[:SIDE, :]

    @pl.when(step == 0)
    def _():
        loss_out[...] = line

    @pl.when(step > 0)
    def _():
        loss_out[...] += line

    @pl.when(step == owned - 1)
    def _():
        back[...] = matmul(all_picks(side, owned, rows, capacity), held[...], 0, 0).astype(BF16)


def back_kernel(capacity, owned, side, grads, slab, back, held):
    step = pl.program_id(0)
    rows = grads.shape[0]
    here = pl.ds(pl.multiple_of(step * rows, rows), rows)
    held[here, :] = matmul(grads[...], slab[...]).astype(BF16)

    @pl.when(step == owned - 1)
    def _():
        back[...] = matmul(all_picks(side, owned, rows, capacity), held[...], 0, 0).astype(BF16)


def head_kernel(rows_a, rows_b, grads, out):
    split = rows_a.shape[1]
    out[:, :split] = matmul(grads[...], rows_a[...], 0, 0).astype(BF16)
    out[:, split:] = matmul(grads[...], rows_b[...], 0, 0).astype(BF16)


def combine_kernel(capacity, info, part_a, part_b, losses, hidden_out, loss_out):
    split = part_a.shape[1]
    picks = placing(info, capacity, part_a.shape[0])
    hidden_out[:, :split] = matmul(picks, part_a[...], 0, 0).astype(BF16)
    hidden_out[:, split:] = matmul(picks, part_b[...], 0, 0).astype(BF16)
    loss_out[...] = matmul(losses[...].astype(BF16), picks)[0:1, :].astype(BF16)


def exchanged(capacity, devices, info, side, hidden, head_weight, blocks):
    tokens, features = hidden.shape
    split = features // 4 * 3
    rest = features - split
    slab_rows = SB * BLOCK
    owned = head_weight.shape[0] // slab_rows
    rows = devices * CAP
    buffer_rows = devices * capacity
    places = owned * rows
    params = pltpu.CompilerParams(vmem_limit_bytes=VMEM)

    def shape(*dims, dtype=BF16):
        return jax.ShapeDtypeStruct(dims, dtype)

    def cost(macs, moved):
        return pl.CostEstimate(flops=2 * macs, bytes_accessed=moved, transcendentals=0)

    def whole(height, width):
        return pl.BlockSpec((height, width), lambda s, *_: (0, 0))

    def per_slot(height, width):
        return pl.BlockSpec((height, width), lambda s, *_: (s, 0))

    def exchange(values):
        shaped = values.reshape(devices, capacity, values.shape[1])
        return lax.all_to_all(shaped, AXES, split_axis=0, concat_axis=0, tiled=True).reshape(
            values.shape
        )

    def exchange_side(values):
        shaped = values.reshape(values.shape[0], devices, capacity)
        return lax.all_to_all(shaped, AXES, split_axis=1, concat_axis=1, tiled=True).reshape(
            values.shape
        )

    slab_a = per_slot(slab_rows, split)
    slab_b = pl.BlockSpec((slab_rows, rest), lambda s, *_: (s, split // rest))
    out_a, out_b, side_out = pl.pallas_call(
        functools.partial(send_kernel, capacity),
        out_shape=[
            shape(buffer_rows, split),
            shape(buffer_rows, rest),
            shape(SIDE, buffer_rows, dtype=F32),
        ],
        compiler_params=params,
        cost_estimate=cost(buffer_rows * tokens * features, 8 << 20),
    )(info, hidden, side)
    in_side = exchange_side(side_out[:4])
    in_a = exchange(out_a)
    in_b = exchange(out_b)
    partial, rows_a = pl.pallas_call(
        functools.partial(logits_kernel, capacity),
        out_shape=[shape(places, slab_rows, dtype=F32), shape(places, split)],
        grid=(owned,),
        in_specs=[whole(4, buffer_rows), whole(buffer_rows, split), slab_a],
        out_specs=[per_slot(rows, slab_rows), per_slot(rows, split)],
        compiler_params=params,
        cost_estimate=cost(2 * places * slab_rows * split, 40 << 20),
    )(in_side, in_a, head_weight)
    rows_b, grads, back_b, losses = pl.pallas_call(
        functools.partial(loss_kernel, capacity, owned),
        out_shape=[
            shape(places, rest),
            shape(places, slab_rows),
            shape(buffer_rows, rest),
            shape(SIDE, buffer_rows, dtype=F32),
        ],
        grid_spec=pltpu.PrefetchScalarGridSpec(
            num_scalar_prefetch=1,
            grid=(owned,),
            in_specs=[
                whole(4, buffer_rows),
                whole(buffer_rows, rest),
                slab_b,
                per_slot(rows, slab_rows),
            ],
            out_specs=[
                per_slot(rows, rest),
                per_slot(rows, slab_rows),
                whole(buffer_rows, rest),
                whole(SIDE, buffer_rows),
            ],
            scratch_shapes=[pltpu.VMEM((places, rest), BF16)],
        ),
        compiler_params=params,
        cost_estimate=cost(2 * places * slab_rows * rest, 16 << 20),
    )(blocks, in_side, in_b, head_weight, partial)
    got_b = exchange(back_b)
    got_loss = exchange_side(losses[:1])
    back_a = pl.pallas_call(
        functools.partial(back_kernel, capacity, owned),
        out_shape=shape(buffer_rows, split),
        grid=(owned,),
        in_specs=[whole(4, buffer_rows), per_slot(rows, slab_rows), slab_a],
        out_specs=whole(buffer_rows, split),
        scratch_shapes=[pltpu.VMEM((places, split), BF16)],
        compiler_params=params,
        cost_estimate=cost(2 * places * slab_rows * split, 40 << 20),
    )(in_side, grads, head_weight)
    got_a = exchange(back_a)
    head_grad = pl.pallas_call(
        head_kernel,
        out_shape=shape(*head_weight.shape),
        grid=(owned,),
        in_specs=[per_slot(rows, split), per_slot(rows, rest), per_slot(rows, slab_rows)],
        out_specs=per_slot(slab_rows, features),
        compiler_params=params,
        cost_estimate=cost(places * slab_rows * features, 40 << 20),
    )(rows_a, rows_b, grads)
    hidden_grad, token_loss = pl.pallas_call(
        functools.partial(combine_kernel, capacity),
        out_shape=[shape(tokens, features), shape(1, tokens)],
        compiler_params=params,
        cost_estimate=cost(buffer_rows * tokens * features, 8 << 20),
    )(info, got_a, got_b, got_loss)
    return hidden_grad, token_loss.reshape(tokens), head_grad


def shards(
    hidden, head_weight, language_blocks, language_owner, token_language, labels, loss_weight
):
    devices = lax.axis_size("vocab") * lax.axis_size("fsdp")
    languages = language_owner.shape[0]
    tokens = hidden.shape[0]
    owned = languages // devices
    most = owned * CAP
    info, side = pl.pallas_call(
        functools.partial(place_kernel, owned),
        out_shape=[
            jax.ShapeDtypeStruct((SIDE, tokens), jnp.int32),
            jax.ShapeDtypeStruct((SIDE, tokens), BF16),
        ],
    )(
        token_language,
        token_language.reshape(1, tokens),
        language_owner[:, None],
        language_owner[None, :],
        labels[None, :],
        loss_weight[None, :],
    )
    self_index = lax.axis_index(AXES)
    own_slots = self_index * owned + jnp.arange(owned, dtype=jnp.int32)
    owns = (own_slots[:, None] == language_owner[None, :]).astype(jnp.int32)
    blocks = jnp.sum(owns[:, :, None] * language_blocks[None], axis=1).reshape(-1)
    values = (info, side, hidden, head_weight, blocks)
    full = functools.partial(exchanged, most, devices)
    if most % 32:
        return full(*values)
    packed = most // 4 * 3
    longest = lax.pmax(jnp.max(info[1]), AXES)
    return lax.cond(longest < packed, functools.partial(exchanged, packed, devices), full, *values)


def solution(mesh):
    in_specs = (
        P(AXES, None),
        P(AXES, None),
        P(),
        P(),
        P(AXES, None),
        P(AXES),
        P(AXES),
    )
    out_specs = (P(AXES, None), P(AXES), P(AXES, None))
    return jax.shard_map(shards, mesh=mesh, in_specs=in_specs, out_specs=out_specs, check_vma=False)
```
